128 devices in a mesh: expert: 8 (over y, core), tensor: 16 (over z, x).
Axes of the slice: x: 4, y: 4, z: 4, core: 2. Of those that a mesh axis runs over, the one named last changes fastest.
Arguments:
- tokens: bfloat16 [4096, 4096], P(('expert', 'tensor')), may hold values from -6 to 6
- expert_ids: int32 [4096, 2], P(('expert', 'tensor')), may hold values from 0 to 15, as said below
- slots: int32 [4096, 2], P(('expert', 'tensor')), may hold values from 0 to 7, as said below
- combine_weights: float32 [4096, 2], P(('expert', 'tensor')), may hold values from 0.25 to 1
- big_gate: bfloat16 [8, 4096, 14336], P('expert', None, 'tensor'), may hold values from -0.09375 to 0.09375
- big_up: bfloat16 [8, 4096, 14336], P('expert', None, 'tensor'), may hold values from -0.09375 to 0.09375
- big_down: bfloat16 [8, 14336, 4096], P('expert', 'tensor'), may hold values from -0.046875 to 0.046875
- small_gate: bfloat16 [8, 4096, 1792], P('expert', 'tensor'), may hold values from -0.09375 to 0.09375
- small_up: bfloat16 [8, 4096, 1792], P('expert', 'tensor'), may hold values from -0.09375 to 0.09375
- small_down: bfloat16 [8, 1792, 4096], P('expert', None, 'tensor'), may hold values from -0.125 to 0.125
Outputs:
- mixed: bfloat16 [4096, 4096], P(('expert', 'tensor'))
The draws below stay inside these ranges and needn't reach their ends.
Inputs may be any that keep to these rules, and one draw needn't show every extreme that they name: `expert_ids`: each token names two different experts; an id below 8 is the big expert of that group index, an id of 8 or more is the small expert of group index id - 8. In each aligned block of 32 rows (the rows of one device) no expert is named more than 8 times, and at least one expert, the same for all blocks, is named exactly 8 times in every block. Within each aligned block of 32 rows, the choices that name one expert hold distinct slots.
All inputs are finite; a program needn't handle non-finite values.
Results may differ from the reference program's by a relative error of at most 0.025.
Values may be sent and summed in bfloat16 or wider, within the bound.
A program may use at most 128 MiB of HBM per device.

```python
import jax
import jax.numpy as jnp
from jax import lax

D = 4096
FF_B = 14336
FF_S = 1792
TOK_DEV = 32
NB = 8
NS = 8
EXPERT_TOTAL = 16
CAP = 8
BLOCKS = 128
TOKENS = 4096
N_TENSOR = 16


def routing(key):
    blocks = TOKENS // TOK_DEV
    candidate_experts = EXPERT_TOTAL * CAP
    popular_key, extra_score_key, selection_key, ordering_key, position_key = jax.random.split(key, 5)
    preferred_experts = jax.random.randint(popular_key, (), 0, EXPERT_TOTAL)
    extra_score = jax.random.randint(extra_score_key, (EXPERT_TOTAL,), 0, 4)
    expert_range = jnp.arange(EXPERT_TOTAL)
    extra_score = jnp.where(expert_range == preferred_experts, 4, extra_score)
    extra_score = jnp.where(expert_range == EXPERT_TOTAL - 1, 4, extra_score)
    candidate_expert = jnp.arange(candidate_experts, dtype=jnp.int32) // CAP
    router_scores = jax.random.randint(selection_key, (blocks, candidate_experts), 0, 2 ** 18)
    key_sorted = (extra_score[candidate_expert][None, :] * 2 ** 18 + router_scores) * candidate_experts + jnp.arange(candidate_experts, dtype=jnp.int32)[None, :]
    _, chosen = lax.top_k(key_sorted, 2 * TOK_DEV)
    labels = jnp.sort(chosen // CAP, axis=1)
    pairs = jnp.stack([labels[:, :TOK_DEV], labels[:, TOK_DEV:]], axis=2)
    shuffle = jax.random.randint(ordering_key, (blocks, TOK_DEV), 0, 2 ** 16) * TOK_DEV + jnp.arange(TOK_DEV, dtype=jnp.int32)[None, :]
    order = jnp.argsort(shuffle, axis=1, stable=True)
    ids = jnp.take_along_axis(pairs, order[:, :, None], axis=1).reshape(blocks, 2 * TOK_DEV)
    onehot = (ids[:, :, None] == jnp.arange(EXPERT_TOTAL, dtype=jnp.int32)[None, None, :]).astype(jnp.int32)
    ranks = jnp.sum(onehot * (jnp.cumsum(onehot, axis=1) - 1), axis=2)
    table_keys = jax.random.randint(position_key, (blocks, EXPERT_TOTAL, CAP), 0, 2 ** 16) * CAP + jnp.arange(CAP, dtype=jnp.int32)[None, None, :]
    tables = jnp.argsort(table_keys, axis=2, stable=True).astype(jnp.int32).reshape(blocks, candidate_experts)
    slot_values = jnp.take_along_axis(tables, ids * CAP + ranks, axis=1)
    return (ids.reshape(TOKENS, 2).astype(jnp.int32), slot_values.reshape(TOKENS, 2).astype(jnp.int32))


def draw_expert_ids(key, part):
    chosen_ids, _ = routing(key)
    return chosen_ids


def draw_slots(key, part):
    _, slot_values = routing(key)
    return slot_values


def level_of(stream_key, extent, cuts, smallest, high):
    loudness, own = 1.0, jax.random.fold_in(stream_key, 6)
    for position, parts in cuts:
        steps = jnp.exp(jax.random.uniform(jax.random.fold_in(own, position), (parts,), jnp.float32, smallest / len(cuts), high / len(cuts)))
        loudness = loudness * jnp.repeat(steps, extent[position] // parts).reshape([-1 if axis == position else 1 for axis in range(len(extent))])
    return loudness


def noise(own_key, dims, spread, most, pieces=(), kind=jnp.bfloat16):
    loudness = level_of(own_key, dims, pieces, -0.22, 0.18) if pieces else 1.0
    drawn = jax.random.normal(own_key, dims, jnp.float32) * spread * loudness
    return jnp.minimum(jnp.maximum(drawn, -most), most).astype(kind)


def setup_inputs(seed: int = 0) -> dict:
    seeds = jax.random.split(jax.random.key(seed), 11)
    return {
        "tokens": noise(seeds[0], (TOKENS, D), 1.0, 6.0, ((0, 128),)),
        "expert_ids": draw_expert_ids(jax.random.fold_in(seeds[10], 71), 0),
        "slots": draw_slots(jax.random.fold_in(seeds[10], 71), 0),
        "combine_weights": jnp.clip(0.25 + 0.75 * jax.random.uniform(seeds[3], (TOKENS, 2), jnp.float32) ** level_of(seeds[3], (TOKENS, 2), ((0, 128),), -0.2, 0.2), 0.25, 1.0),
        "big_gate": noise(seeds[4], (NB, D, FF_B), D ** -0.5, 0.09375, ((0, 8), (2, 16))),
        "big_up": noise(seeds[5], (NB, D, FF_B), D ** -0.5, 0.09375, ((0, 8), (2, 16))),
        "big_down": noise(seeds[6], (NB, FF_B, D), FF_B ** -0.5, 0.046875, ((0, 8), (1, 16))),
        "small_gate": noise(seeds[7], (NS, D, FF_S), D ** -0.5, 0.09375, ((0, 8), (1, 16))),
        "small_up": noise(seeds[8], (NS, D, FF_S), D ** -0.5, 0.09375, ((0, 8), (1, 16))),
        "small_down": noise(seeds[9], (NS, FF_S, D), FF_S ** -0.5, 0.125, ((0, 8), (2, 16))),
    }


def dispatch_block(flat_block, rows, positions):
    first = (flat_block[None, :, 0] == positions[:, None]).astype(jnp.float32)
    second = (flat_block[None, :, 1] == positions[:, None]).astype(jnp.float32)
    onehot = (first + second).astype(jnp.bfloat16)
    return jnp.dot(onehot, rows, preferred_element_type=jnp.float32).astype(jnp.bfloat16)


def big_expert(operands):
    rows, w_gate, w_up, w_down = operands
    rows = rows.reshape(-1, D)
    gate = jnp.dot(rows, w_gate, preferred_element_type=jnp.float32)
    up = jnp.dot(rows, w_up, preferred_element_type=jnp.float32)
    hidden = (jax.nn.silu(gate) * up).astype(jnp.bfloat16)
    piece = FF_B // N_TENSOR

    def add_piece(index, total):
        start = (index * piece).astype(jnp.int32)
        left = lax.dynamic_slice_in_dim(hidden, start, piece, 1)
        right = lax.dynamic_slice_in_dim(w_down, start, piece, 0)
        term = jnp.dot(left, right, preferred_element_type=jnp.float32).astype(jnp.bfloat16)
        return total + lax.optimization_barrier(term).astype(jnp.float32)

    total = lax.fori_loop(0, N_TENSOR, add_piece, jnp.zeros((rows.shape[0], D), jnp.float32))
    return total.astype(jnp.bfloat16).reshape(BLOCKS, CAP, D)


def small_expert(operands):
    rows, w_gate, w_up, w_down = operands
    rows = rows.reshape(-1, D)
    piece = D // N_TENSOR

    def add_piece(index, totals):
        start = (index * piece).astype(jnp.int32)
        left = lax.dynamic_slice_in_dim(rows, start, piece, 1)
        gate_rows = lax.dynamic_slice_in_dim(w_gate, start, piece, 0)
        up_rows = lax.dynamic_slice_in_dim(w_up, start, piece, 0)
        gate_term = jnp.dot(left, gate_rows, preferred_element_type=jnp.float32).astype(jnp.bfloat16)
        up_term = jnp.dot(left, up_rows, preferred_element_type=jnp.float32).astype(jnp.bfloat16)
        gate_term, up_term = lax.optimization_barrier((gate_term, up_term))
        return (totals[0] + gate_term.astype(jnp.float32), totals[1] + up_term.astype(jnp.float32))

    empty = jnp.zeros((rows.shape[0], FF_S), jnp.float32)
    gate, up = lax.fori_loop(0, N_TENSOR, add_piece, (empty, empty))
    hidden = (jax.nn.silu(gate) * up).astype(jnp.bfloat16)
    output = jnp.dot(hidden, w_down, preferred_element_type=jnp.float32).astype(jnp.bfloat16)
    return output.reshape(BLOCKS, CAP, D)


def reference(tokens, expert_ids, slots, combine_weights, big_gate, big_up, big_down, small_gate, small_up, small_down):
    flat = (expert_ids.astype(jnp.int32) * CAP + slots.astype(jnp.int32)).reshape(BLOCKS, TOK_DEV, 2)
    rows = tokens.reshape(BLOCKS, TOK_DEV, D)
    positions = jnp.arange(EXPERT_TOTAL * CAP, dtype=jnp.int32)
    dispatched = lax.map(lambda pair: dispatch_block(pair[0], pair[1], positions), (flat, rows))
    dispatched = jnp.moveaxis(dispatched.reshape(BLOCKS, EXPERT_TOTAL, CAP, D), 1, 0)
    big_out = lax.map(big_expert, (dispatched[:NB], big_gate, big_up, big_down))
    small_out = lax.map(small_expert, (dispatched[NB:], small_gate, small_up, small_down))
    returned = jnp.concatenate([big_out, small_out], axis=0)
    returned = jnp.moveaxis(returned, 0, 1).reshape(BLOCKS, EXPERT_TOTAL * CAP, D)
    first = jnp.take_along_axis(returned, flat[:, :, 0][:, :, None], axis=1).astype(jnp.float32)
    second = jnp.take_along_axis(returned, flat[:, :, 1][:, :, None], axis=1).astype(jnp.float32)
    weights = combine_weights.reshape(BLOCKS, TOK_DEV, 2)
    mixed = weights[:, :, 0:1] * first + weights[:, :, 1:2] * second
    return mixed.astype(jnp.bfloat16).reshape(TOKENS, D)
```

```python
import functools

import jax
import jax.numpy as jnp
from jax import lax
from jax.experimental import pallas as pl
from jax.experimental.pallas import tpu as pltpu
from jax.sharding import PartitionSpec as P

F32, BF16 = jnp.float32, jnp.bfloat16
MESH = pl.DeviceIdType.MESH
TILE = 256
AXES = (("x", "z"), ("z", "x"))


def add_into(dst, parts, rows, width):
    step = min(width, 512)

    @pl.loop(0, width // step)
    def _(c):
        cols = pl.ds(pl.multiple_of(c * step, step), step)
        total = dst[:, cols].astype(F32)
        for part in parts:
            total += part[:, cols].astype(F32)
        dst[:, cols] = total.astype(BF16)


class Copies:
    def __init__(self, send, recv):
        self.send, self.recv, self.used = send, recv, 0

    def __call__(self, src, dst, device):
        k = self.used
        self.used += 1
        return pltpu.make_async_remote_copy(
            src_ref=src, dst_ref=dst, send_sem=self.send.at[k], recv_sem=self.recv.at[k],
            device_id=device, device_id_type=MESH,
        )


class Gather:
    def __init__(self, copies, neighbour, buf):
        self.c = c = {}
        for h, (first, second) in enumerate(AXES):
            def row(g, r, lo=0, n=32):
                return buf.at[g, pl.ds(128 * h + 32 * r + lo, n)]

            c[h, "a", 1] = copies(row(0, 0), row(0, 3), neighbour(first, 1))
            c[h, "a", 3] = copies(row(0, 0), row(0, 1), neighbour(first, 3))
            c[h, "f", 1] = copies(row(0, 3, 0, 16), row(0, 2, 0, 16), neighbour(first, 1))
            c[h, "f", 3] = copies(row(0, 1, 16, 16), row(0, 2, 16, 16), neighbour(first, 3))
            for r in range(4):
                c[h, "b", 1, r] = copies(row(0, r), row(3, r), neighbour(second, 1))
                c[h, "b", 3, r] = copies(row(0, r), row(1, r), neighbour(second, 3))
            for r in (0, 1):
                c[h, "g", 1, r] = copies(row(3, r), row(2, r), neighbour(second, 1))
            for r in (2, 3):
                c[h, "g", 3, r] = copies(row(1, r), row(2, r), neighbour(second, 3))

    def step(self, number):
        c = self.c
        for h in (0, 1):
            def go(*keys):
                for key in keys:
                    c[(h, *key)].start()

            def got(*keys):
                for key in keys:
                    c[(h, *key)].wait_recv()

            if number == 0:
                go(("a", 1), ("a", 3), ("b", 1, 0), ("b", 3, 0))
            elif number == 1:
                got(("a", 1))
                go(("f", 1), ("b", 1, 3), ("b", 3, 3))
                got(("a", 3))
                go(("f", 3), ("b", 1, 1), ("b", 3, 1))
            elif number == 2:
                got(("b", 1, 0))
                go(("g", 1, 0))
            elif number == 3:
                got(("f", 1), ("f", 3))
                go(("b", 1, 2), ("b", 3, 2))
            elif number == 4:
                got(("b", 1, 1))
                go(("g", 1, 1))
                got(("b", 3, 3))
                go(("g", 3, 3))
            elif number == 5:
                got(("b", 3, 2))
                go(("g", 3, 2))
            else:
                got(("b", 1, 2), ("b", 1, 3), ("b", 3, 0), ("b", 3, 1))
                got(("g", 1, 0), ("g", 1, 1), ("g", 3, 2), ("g", 3, 3))

    def sent(self):
        for copy in self.c.values():
            copy.wait_send()


class Scatter:
    def __init__(self, copies, neighbour, row, width, o, n, o2, n2):
        self.row, self.width = row, width
        self.o, self.n, self.o2, self.n2 = o, n, o2, n2
        self.c = c = {}
        for h, (second, first) in enumerate(AXES):
            b = 128 * h
            c[h, "o", 1] = copies(row(2, b, 64), o.at[h, 0], neighbour(first, 1))
            c[h, "o", 3] = copies(row(2, b + 64, 64), o.at[h, 1], neighbour(first, 3))
            c[h, "e", 1] = copies(row(1, b + 64, 64), n.at[h, 0, pl.ds(64, 64)], neighbour(first, 1))
            c[h, "e", 3] = copies(row(3, b, 64), n.at[h, 1, pl.ds(0, 64)], neighbour(first, 3))
            c[h, "l", 1] = copies(row(1, b, 64), n.at[h, 0, pl.ds(0, 64)], neighbour(first, 1))
            c[h, "l", 3] = copies(row(3, b + 64, 64), n.at[h, 1, pl.ds(64, 64)], neighbour(first, 3))
            c[h, "p", 1] = copies(row(0, b + 64, 16), o2.at[h, 0], neighbour(second, 1))
            c[h, "p", 3] = copies(row(0, b + 80, 16), o2.at[h, 1], neighbour(second, 3))
            c[h, "q", 1] = copies(row(0, b + 32, 32), n2.at[h, 0], neighbour(second, 1))
            c[h, "q", 3] = copies(row(0, b + 96, 32), n2.at[h, 1], neighbour(second, 3))

    def opposite(self):
        for h in (0, 1):
            self.c[h, "o", 1].start()
            self.c[h, "o", 3].start()

    def early(self, way):
        for h in (0, 1):
            self.c[h, "e", way].start()

    def step(self, number):
        c, row, width = self.c, self.row, self.width
        for h in (0, 1):
            b = 128 * h
            if number == 1:
                c[h, "o", 1].wait_recv()
                add_into(row(1, b, 64), [self.o.at[h, 0]], 64, width)
                c[h, "l", 1].start()
                c[h, "o", 3].wait_recv()
                add_into(row(3, b + 64, 64), [self.o.at[h, 1]], 64, width)
                c[h, "l", 3].start()
            elif number == 2:
                for way in (1, 3):
                    c[h, "e", way].wait_recv()
                    c[h, "l", way].wait_recv()
                add_into(row(0, b, 128), [self.n.at[h, 0], self.n.at[h, 1]], 128, width)
                c[h, "p", 1].start()
                c[h, "p", 3].start()
            elif number == 3:
                c[h, "p", 1].wait_recv()
                add_into(row(0, b + 32, 16), [self.o2.at[h, 0]], 16, width)
                c[h, "q", 1].start()
                c[h, "p", 3].wait_recv()
                add_into(row(0, b + 112, 16), [self.o2.at[h, 1]], 16, width)
                c[h, "q", 3].start()
            else:
                c[h, "q", 1].wait_recv()
                c[h, "q", 3].wait_recv()

    def total(self, h, cols):
        own = self.row(0, 128 * h, 32)[:, cols].astype(F32)
        return own + self.n2[h, 0, :, cols].astype(F32) + self.n2[h, 1, :, cols].astype(F32)

    def sent(self):
        for copy in self.c.values():
            copy.wait_send()


def kernel(
    ids, slots, weights, tokens, big_gate, big_up, big_down, small_gate, small_up, small_down,
    out,
    pk, dr, hm, xg, wgu, wd, hid, ob, nb, o2b, n2b, rb,
    sr, sc, sg, su, sd, ps, osm, ns, o2s, n2s, ah, back, sb,
    send, recv, local, tile_sem,
):
    width = tokens.shape[1]
    hidden = wd.shape[0]
    small = sg.shape[1]
    blocks = width // TILE
    half = width // 2
    e = lax.axis_index("expert")
    t = lax.axis_index("tensor")
    z, x = lax.div(t, 4), lax.rem(t, 4)

    def place(sz, sx):
        return lax.rem(z + sz, 4) * 4 + lax.rem(x + sx, 4)

    def peer(sz, sx):
        return {"tensor": place(sz, sx)}

    def neighbour(axis, s):
        return peer(s, 0) if axis == "z" else peer(0, s)

    offsets = [(sz, sx) for sz in range(4) for sx in range(4) if (sz, sx) != (0, 0)]

    barrier = pltpu.get_barrier_semaphore()
    for s in range(1, 8):
        pl.semaphore_signal(barrier, inc=1, device_id={"expert": lax.rem(e + s, 8)}, device_id_type=MESH)
    for sz, sx in offsets:
        pl.semaphore_signal(barrier, inc=1, device_id=peer(sz, sx), device_id_type=MESH)

    loads = [
        pltpu.make_async_copy(src, dst, local.at[k])
        for k, (src, dst) in enumerate(
            ((small_gate, sg), (small_up, su), (big_down, wd), (small_down, sd))
        )
    ]
    for load in loads:
        load.start()

    def tile_loads(j, slot):
        cols = pl.ds(pl.multiple_of(j * 128, 128), 128)
        return (
            pltpu.make_async_copy(big_gate.at[:, cols], wgu.at[slot, :, pl.ds(0, 128)], tile_sem.at[slot, 0]),
            pltpu.make_async_copy(big_up.at[:, cols], wgu.at[slot, :, pl.ds(128, 128)], tile_sem.at[slot, 1]),
        )

    for load in tile_loads(0, 0):
        load.start()

    where = (ids[...] & 7) * 16 + (ids[...] >> 3) * 8 + slots[...]
    spot = lax.broadcasted_iota(jnp.int32, (128, tokens.shape[0]), 0)
    first, second = spot == where[0:1, :], spot == where[1:2, :]
    onehot = (first.astype(F32) + second.astype(F32)).astype(BF16)

    @pl.loop(0, blocks)
    def _(c):
        cols = pl.ds(pl.multiple_of(c * TILE, TILE), TILE)
        rows = jnp.dot(onehot, tokens[:, cols], preferred_element_type=F32)
        pk[:, :, cols] = rows.astype(BF16).reshape(8, 16, TILE)

    pl.semaphore_wait(barrier, 22)

    copies = Copies(send, recv)
    dispatch = []
    for s in range(1, 8):
        to = lax.rem(e + s, 8)
        dispatch.append(copies(pk.at[to], dr.at[e], {"expert": to}))
    for copy in dispatch:
        copy.start()
    dr[e] = pk[e]

    out_row = lax.broadcasted_iota(jnp.int32, (128, 128), 0)
    in_row = lax.broadcasted_iota(jnp.int32, (128, 128), 1)
    from_row = ((out_row & 63) >> 3) * 16 + (out_row >> 6) * 8 + (out_row & 7)
    by_kind = (from_row == in_row).astype(F32).astype(BF16)
    back_row = (in_row & 63) >> 3
    back_row = back_row * 16 + (in_row >> 6) * 8 + (in_row & 7)
    by_group = (back_row == out_row).astype(F32).astype(BF16)

    for copy in dispatch:
        copy.wait_recv()

    @pl.loop(0, blocks)
    def _(c):
        cols = pl.ds(pl.multiple_of(c * TILE, TILE), TILE)
        rows = dr[:, :, cols].reshape(128, TILE)
        rows = jnp.dot(by_kind, rows, preferred_element_type=F32).astype(BF16)
        xg[0, 0:32, cols] = rows[0:32]
        xg[0, 128:160, cols] = rows[32:64]
        sr[c] = rows[64:128]

    columns = []
    for sz, sx in offsets:
        rel = (-sz) % 4 * 4 + (-sx) % 4
        columns.append(copies(sr.at[place(sz, sx)], sc.at[rel], peer(sz, sx)))
    for copy in columns:
        copy.start()
    sc[0] = sr[t]

    gather = Gather(copies, neighbour, xg)
    gather.step(0)
    gather.step(1)

    small_sum = Scatter(
        copies, neighbour, lambda g, lo, n: ps.at[g, pl.ds(lo, n)], 2 * small, osm, ns, o2s, n2s
    )

    def small_terms(g):
        rows = jnp.concatenate(
            [sc[4 * g + r, 0:32] for r in range(4)] + [sc[4 * r + g, 32:64] for r in range(4)], axis=0
        )

        @pl.loop(0, small // TILE)
        def _(c):
            cols = pl.ds(pl.multiple_of(c * TILE, TILE), TILE)
            far = pl.ds(pl.multiple_of(small + c * TILE, TILE), TILE)
            ps[g, :, cols] = jnp.dot(rows, sg[:, cols], preferred_element_type=F32).astype(BF16)
            ps[g, :, far] = jnp.dot(rows, su[:, cols], preferred_element_type=F32).astype(BF16)

    for load in loads[:2]:
        load.wait()
    for copy in columns:
        copy.wait_recv()
    small_terms(2)
    small_sum.opposite()
    gather.step(2)
    small_terms(1)
    small_sum.early(1)
    small_terms(3)
    small_sum.early(3)
    gather.step(3)
    small_terms(0)
    gather.step(4)
    gather.step(5)
    small_sum.step(1)
    gather.step(6)

    def big_hidden(lo, hi):
        @pl.loop(lo, hi)
        def _(j):
            slot = lax.rem(j, 2)
            for load in tile_loads(j, slot):
                load.wait()

            @pl.when(j + 1 < hidden // 128)
            def _():
                for load in tile_loads(j + 1, 1 - slot):
                    load.start()

            cols = pl.ds(pl.multiple_of(j * 128, 128), 128)

            @pl.loop(0, 4)
            def _(g):
                both = jnp.dot(xg[g], wgu[slot], preferred_element_type=F32)
                gate, up = both[:, :128], both[:, 128:]
                hid[g, :, cols] = (gate / (1.0 + jnp.exp(-gate)) * up).astype(BF16)

    tiles = hidden // 128
    marks = [0, tiles * 2 // 7, tiles * 4 // 7, tiles * 6 // 7, tiles]
    big_hidden(marks[0], marks[1])
    small_sum.step(2)
    big_hidden(marks[1], marks[2])
    small_sum.step(3)
    big_hidden(marks[2], marks[3])
    small_sum.step(4)

    for h in (0, 1):
        @pl.loop(0, small // TILE)
        def _(c):
            cols = pl.ds(pl.multiple_of(c * TILE, TILE), TILE)
            far = pl.ds(pl.multiple_of(small + c * TILE, TILE), TILE)
            gate, up = small_sum.total(h, cols), small_sum.total(h, far)
            ah[0, pl.ds(128 * h, 32), cols] = (gate / (1.0 + jnp.exp(-gate)) * up).astype(BF16)

    act = Gather(copies, neighbour, ah)
    act.step(0)
    big_hidden(marks[3], marks[4])
    act.step(1)

    gather.sent()
    loads[2].wait()

    def big_terms(g, q):
        @pl.loop(q * half // TILE, (q + 1) * half // TILE)
        def _(c):
            cols = pl.ds(pl.multiple_of(c * TILE, TILE), TILE)
            xg[g, :, cols] = jnp.dot(hid[g], wd[:, cols], preferred_element_type=F32).astype(BF16)

    def big_scatter(q):
        def row(g, lo, n):
            return xg.at[g, pl.ds(lo, n), pl.ds(q * half, half)]

        return Scatter(copies, neighbour, row, half, ob.at[q], nb.at[q], o2b.at[q], n2b.at[q])

    sums = []
    for q in (0, 1):
        sums.append(big_scatter(q))
        big_terms(2, q)
        sums[q].opposite()
        big_terms(1, q)
        sums[q].early(1)
        big_terms(3, q)
        sums[q].early(3)
        big_terms(0, q)
        act.step(2 + 2 * q)
        act.step(3 + 2 * q)

    sums[0].step(1)
    act.step(6)
    loads[3].wait()
    for g in range(4):
        rows = jnp.dot(ah[g], sd[...], preferred_element_type=F32).astype(BF16)
        for r in range(4):
            back[4 * g + r, 0:32] = rows[32 * r:32 * r + 32]
            back[4 * r + g, 32:64] = rows[128 + 32 * r:160 + 32 * r]
    home = []
    for sz, sx in offsets:
        home.append(copies(back.at[4 * sz + sx], sb.at[t], peer(sz, sx)))
    for copy in home:
        copy.start()
    sb[t] = back[0]

    sums[1].step(1)
    for number in (2, 3, 4):
        for q in (0, 1):
            sums[q].step(number)
    for q in (0, 1):
        for h in (0, 1):
            @pl.loop(0, half // TILE)
            def _(c):
                cols = pl.ds(pl.multiple_of(c * TILE, TILE), TILE)
                far = pl.ds(pl.multiple_of(q * half + c * TILE, TILE), TILE)
                rb[pl.ds(32 * h, 32), far] = sums[q].total(h, cols).astype(BF16)

    for copy in home:
        copy.wait_recv()
    for copy in dispatch:
        copy.wait_send()

    @pl.loop(0, blocks)
    def _(c):
        cols = pl.ds(pl.multiple_of(c * TILE, TILE), TILE)
        rows = jnp.concatenate([rb[:, cols], sb[c]], axis=0)
        rows = jnp.dot(by_group, rows, preferred_element_type=F32).astype(BF16)
        pk[:, :, cols] = rows.reshape(8, 16, TILE)

    returned = []
    for s in range(1, 8):
        to = lax.rem(e + s, 8)
        returned.append(copies(pk.at[to], hm.at[e], {"expert": to}))
    for copy in returned:
        copy.start()
    hm[e] = pk[e]

    mix = jnp.where(first, weights[0:1, :], 0.0) + jnp.where(second, weights[1:2, :], 0.0)
    mix = mix.T
    coarse = mix.astype(BF16)
    fine = (mix - coarse.astype(F32)).astype(BF16)

    for copy in returned:
        copy.wait_recv()

    @pl.loop(0, blocks)
    def _(c):
        cols = pl.ds(pl.multiple_of(c * TILE, TILE), TILE)
        rows = hm[:, :, cols].reshape(128, TILE)
        total = jnp.dot(coarse, rows, preferred_element_type=F32)
        total += jnp.dot(fine, rows, preferred_element_type=F32)
        out[:, cols] = total.astype(BF16)

    for copy in columns + home + returned:
        copy.wait_send()
    for group in (small_sum, act, sums[0], sums[1]):
        group.sent()


def shards(
    tokens, expert_ids, slots, combine_weights,
    big_gate, big_up, big_down, small_gate, small_up, small_down,
):
    tok, width = tokens.shape
    hidden = big_gate.shape[2]
    small = small_gate.shape[2]
    half = width // 2
    vmem = pl.BlockSpec(memory_space=pltpu.VMEM)
    hbm = pl.BlockSpec(memory_space=pl.ANY)

    def buf(*shape):
        return pltpu.VMEM(shape, BF16)

    n_copies = 7 + 15 + 32 + 20 + 32 + 40 + 15 + 7
    return pl.pallas_call(
        kernel,
        out_shape=jax.ShapeDtypeStruct((tok, width), BF16),
        in_specs=[vmem] * 4 + [hbm] * 6,
        out_specs=vmem,
        scratch_shapes=[
            buf(8, 16, width), buf(8, 16, width), buf(8, 16, width),
            buf(4, 256, width), buf(2, width, 256), buf(hidden, width), buf(4, 256, hidden),
            buf(2, 2, 2, 64, half), buf(2, 2, 2, 128, half), buf(2, 2, 2, 16, half), buf(2, 2, 2, 32, half),
            buf(64, width),
            buf(16, 64, TILE), buf(16, 64, TILE),
            buf(TILE, small), buf(TILE, small), buf(small, TILE),
            buf(4, 256, 2 * small),
            buf(2, 2, 64, 2 * small), buf(2, 2, 128, 2 * small), buf(2, 2, 16, 2 * small), buf(2, 2, 32, 2 * small),
            buf(4, 256, small), buf(16, 64, TILE), buf(16, 64, TILE),
            pltpu.SemaphoreType.DMA((n_copies,)),
            pltpu.SemaphoreType.DMA((n_copies,)),
            pltpu.SemaphoreType.DMA((4,)),
            pltpu.SemaphoreType.DMA((2, 2)),
        ],
        compiler_params=pltpu.CompilerParams(
            collective_id=0, has_side_effects=True, vmem_limit_bytes=62 * 1024 * 1024
        ),
        cost_estimate=pl.CostEstimate(
            flops=6 * 1024 * width * hidden + 6 * 1024 * TILE * small,
            bytes_accessed=6 * width * hidden + 6 * TILE * small,
            transcendentals=1024 * hidden,
        ),
        name="moe_layer",
    )(
        expert_ids.T, slots.T, combine_weights.T, tokens,
        big_gate[0], big_up[0], big_down[0], small_gate[0], small_up[0], small_down[0],
    )


def solution(mesh):
    return jax.shard_map(
        shards,
        mesh=mesh,
        in_specs=(
            P(("expert", "tensor"), None),
            P(("expert", "tensor"), None),
            P(("expert", "tensor"), None),
            P(("expert", "tensor"), None),
            P("expert", None, "tensor"),
            P("expert", None, "tensor"),
            P("expert", "tensor", None),
            P("expert", "tensor", None),
            P("expert", "tensor", None),
            P("expert", None, "tensor"),
        ),
        out_specs=P(("expert", "tensor"), None),
        check_vma=False,
    )
```

```python
import jax
import jax.numpy as jnp
from jax import lax
from jax.experimental import pallas as pl
from jax.experimental.pallas import tpu as pltpu
from jax.sharding import PartitionSpec as P

F32, BF16 = jnp.float32, jnp.bfloat16
MESH = pl.DeviceIdType.MESH
TILE = 256
AXES = (("x", "z"), ("z", "x"))


def add_into(dst, parts, rows, width):
    step = min(width, 512)

    @pl.loop(0, width // step)
    def _(c):
        cols = pl.ds(pl.multiple_of(c * step, step), step)
        total = dst[:, cols].astype(F32)
        for part in parts:
            total += part[:, cols].astype(F32)
        dst[:, cols] = total.astype(BF16)


class Copies:
    def __init__(self, send, recv):
        self.send, self.recv, self.used = send, recv, 0

    def __call__(self, src, dst, device):
        k = self.used
        self.used += 1
        return pltpu.make_async_remote_copy(
            src_ref=src, dst_ref=dst, send_sem=self.send.at[k], recv_sem=self.recv.at[k],
            device_id=device, device_id_type=MESH,
        )


class Gather:
    def __init__(self, copies, neighbour, buf):
        self.c = c = {}
        for h, (first, second) in enumerate(AXES):
            def row(g, r, lo=0, n=32):
                return buf.at[g, pl.ds(128 * h + 32 * r + lo, n)]

            c[h, "a", 1] = copies(row(0, 0), row(0, 3), neighbour(first, 1))
            c[h, "a", 3] = copies(row(0, 0), row(0, 1), neighbour(first, 3))
            c[h, "f", 1] = copies(row(0, 3, 0, 16), row(0, 2, 0, 16), neighbour(first, 1))
            c[h, "f", 3] = copies(row(0, 1, 16, 16), row(0, 2, 16, 16), neighbour(first, 3))
            for r in range(4):
                c[h, "b", 1, r] = copies(row(0, r), row(3, r), neighbour(second, 1))
                c[h, "b", 3, r] = copies(row(0, r), row(1, r), neighbour(second, 3))
            for r in (0, 1):
                c[h, "g", 1, r] = copies(row(3, r), row(2, r), neighbour(second, 1))
            for r in (2, 3):
                c[h, "g", 3, r] = copies(row(1, r), row(2, r), neighbour(second, 3))

    def step(self, number):
        c = self.c
        for h in (0, 1):
            def go(*keys):
                for key in keys:
                    c[(h, *key)].start()

            def got(*keys):
                for key in keys:
                    c[(h, *key)].wait_recv()

            if number == 0:
                go(("a", 1), ("a", 3), ("b", 1, 0), ("b", 3, 0))
            elif number == 1:
                got(("a", 1))
                go(("f", 1), ("b", 1, 3), ("b", 3, 3))
                got(("a", 3))
                go(("f", 3), ("b", 1, 1), ("b", 3, 1))
            elif number == 2:
                got(("b", 1, 0))
                go(("g", 1, 0))
            elif number == 3:
                got(("f", 1), ("f", 3))
                go(("b", 1, 2), ("b", 3, 2))
            elif number == 4:
                got(("b", 1, 1))
                go(("g", 1, 1))
                got(("b", 3, 3))
                go(("g", 3, 3))
            elif number == 5:
                got(("b", 3, 2))
                go(("g", 3, 2))
            elif number == 6:
                got(("b", 1, 2), ("b", 1, 3), ("b", 3, 0), ("b", 3, 1))
            else:
                got(("g", 1, 0), ("g", 1, 1), ("g", 3, 2), ("g", 3, 3))

    def sent(self, relayed):
        for key, copy in self.c.items():
            if (key[1] == "g") == relayed:
                copy.wait_send()


class LineGather:
    def __init__(self, copies, neighbour, axis, buf, own=None):
        middle = buf.shape[1] // 2
        low, high = pl.ds(0, middle), pl.ds(middle, middle)
        up, down = neighbour(axis, 1), neighbour(axis, 3)
        own = buf.at[0] if own is None else own
        self.out = [copies(own, buf.at[3], up), copies(own, buf.at[1], down)]
        self.on = [
            copies(buf.at[3, low], buf.at[2, low], up), copies(buf.at[1, high], buf.at[2, high], down)
        ]

    def start(self):
        for copy in self.out:
            copy.start()

    def relay(self):
        for first, second in zip(self.out, self.on):
            first.wait_recv()
            second.start()

    def finish(self):
        for copy in self.on:
            copy.wait_recv()

    def sent(self):
        for copy in self.out + self.on:
            copy.wait_send()


class LineScatter:
    def __init__(self, copies, neighbour, axis, buf, o, n):
        low, high = pl.ds(0, 128), pl.ds(128, 128)
        up, down = neighbour(axis, 1), neighbour(axis, 3)
        self.buf, self.o, self.n = buf, o, n
        self.low, self.high = low, high
        self.far = [copies(buf.at[2, low], o.at[0], up), copies(buf.at[2, high], o.at[1], down)]
        self.early = [copies(buf.at[1, high], n.at[0, high], up), copies(buf.at[3, low], n.at[1, low], down)]
        self.late = [copies(buf.at[1, low], n.at[0, low], up), copies(buf.at[3, high], n.at[1, high], down)]

    def relay(self):
        width = self.o.shape[-1]
        self.far[0].wait_recv()
        add_into(self.buf.at[1, self.low], [self.o.at[0]], 128, width)
        self.late[0].start()
        self.far[1].wait_recv()
        add_into(self.buf.at[3, self.high], [self.o.at[1]], 128, width)
        self.late[1].start()

    def finish(self):
        for copy in self.early + self.late:
            copy.wait_recv()

    def total(self, cols):
        return self.buf[0, :, cols].astype(F32) + self.n[0, :, cols].astype(F32) + self.n[1, :, cols].astype(F32)

    def sent(self):
        for copy in self.far + self.early + self.late:
            copy.wait_send()


class Scatter:
    def __init__(self, copies, neighbour, row, width, o, n, o2, n2):
        self.row, self.width = row, width
        self.o, self.n, self.o2, self.n2 = o, n, o2, n2
        self.c = c = {}
        for h, (second, first) in enumerate(AXES):
            b = 128 * h
            c[h, "o", 1] = copies(row(2, b, 64), o.at[h, 0], neighbour(first, 1))
            c[h, "o", 3] = copies(row(2, b + 64, 64), o.at[h, 1], neighbour(first, 3))
            c[h, "e", 1] = copies(row(1, b + 64, 64), n.at[h, 0, pl.ds(64, 64)], neighbour(first, 1))
            c[h, "e", 3] = copies(row(3, b, 64), n.at[h, 1, pl.ds(0, 64)], neighbour(first, 3))
            c[h, "l", 1] = copies(row(1, b, 64), n.at[h, 0, pl.ds(0, 64)], neighbour(first, 1))
            c[h, "l", 3] = copies(row(3, b + 64, 64), n.at[h, 1, pl.ds(64, 64)], neighbour(first, 3))
            c[h, "p", 1] = copies(row(0, b + 64, 16), o2.at[h, 0], neighbour(second, 1))
            c[h, "p", 3] = copies(row(0, b + 80, 16), o2.at[h, 1], neighbour(second, 3))
            c[h, "q", 1] = copies(row(0, b + 32, 32), n2.at[h, 0], neighbour(second, 1))
            c[h, "q", 3] = copies(row(0, b + 96, 32), n2.at[h, 1], neighbour(second, 3))

    def opposite(self):
        for h in (0, 1):
            self.c[h, "o", 1].start()
            self.c[h, "o", 3].start()

    def early(self, way):
        for h in (0, 1):
            self.c[h, "e", way].start()

    def step(self, number):
        c, row, width = self.c, self.row, self.width
        for h in (0, 1):
            b = 128 * h
            if number == 1:
                c[h, "o", 1].wait_recv()
                add_into(row(1, b, 64), [self.o.at[h, 0]], 64, width)
                c[h, "l", 1].start()
                c[h, "o", 3].wait_recv()
                add_into(row(3, b + 64, 64), [self.o.at[h, 1]], 64, width)
                c[h, "l", 3].start()
            elif number == 2:
                for way in (1, 3):
                    c[h, "e", way].wait_recv()
                    c[h, "l", way].wait_recv()
                add_into(row(0, b, 128), [self.n.at[h, 0], self.n.at[h, 1]], 128, width)
                c[h, "p", 1].start()
                c[h, "p", 3].start()
            elif number == 3:
                c[h, "p", 1].wait_recv()
                add_into(row(0, b + 32, 16), [self.o2.at[h, 0]], 16, width)
                c[h, "q", 1].start()
                c[h, "p", 3].wait_recv()
                add_into(row(0, b + 112, 16), [self.o2.at[h, 1]], 16, width)
                c[h, "q", 3].start()
            else:
                c[h, "q", 1].wait_recv()
                c[h, "q", 3].wait_recv()

    def total(self, h, cols):
        own = self.row(0, 128 * h, 32)[:, cols].astype(F32)
        return own + self.n2[h, 0, :, cols].astype(F32) + self.n2[h, 1, :, cols].astype(F32)

    def sent(self):
        for copy in self.c.values():
            copy.wait_send()


def kernel(
    ids, slots, weights, tokens, big_gate, big_up, big_down, small_gate, small_up, small_down,
    out,
    pk, dr, hm, xg, wgu, wd, hid, ob, nb, o2b, n2b,
    sr, xs, wg, wu, wo, ps, op, np_, ac, pd, sb,
    send, recv, local, tile_sem,
):
    width = tokens.shape[1]
    hidden = wd.shape[0]
    tiles = hidden // 128
    blocks = width // TILE
    half = width // 2
    e = lax.axis_index("expert")
    t = lax.axis_index("tensor")
    z, x = lax.div(t, 4), lax.rem(t, 4)

    def peer(sz, sx):
        return {"tensor": lax.rem(z + sz, 4) * 4 + lax.rem(x + sx, 4)}

    def neighbour(axis, s):
        return peer(s, 0) if axis == "z" else peer(0, s)

    barrier = pltpu.get_barrier_semaphore()
    for s in range(1, 8):
        pl.semaphore_signal(barrier, inc=1, device_id={"expert": lax.rem(e + s, 8)}, device_id_type=MESH)
    for s in range(1, 4):
        for axis in ("x", "z"):
            pl.semaphore_signal(barrier, inc=1, device_id=neighbour(axis, s), device_id_type=MESH)

    def units(place):
        return pl.multiple_of(128 * (4 * place - lax.max(place - 1, 0)), 128)

    mine = pl.ds(units(x), 512)
    loads = [
        pltpu.make_async_copy(src, dst, local.at[k])
        for k, (src, dst) in enumerate((
            (small_gate.at[:, mine], wg.at[x]), (small_up.at[:, mine], wu.at[x]),
            (small_down, wo.at[0]), (big_down, wd),
        ))
    ]
    tile_loads = []
    for j in range(tiles):
        cols = pl.ds(j * 128, 128)
        tile_loads.append(pltpu.make_async_copy(big_gate.at[:, cols], wgu.at[j, :, pl.ds(0, 128)], tile_sem.at[j, 0]))
        tile_loads.append(pltpu.make_async_copy(big_up.at[:, cols], wgu.at[j, :, pl.ds(128, 128)], tile_sem.at[j, 1]))
    for load in loads + tile_loads:
        load.start()

    where = (ids[...] & 7) * 16 + (ids[...] >> 3) * 8 + slots[...]
    spot = lax.broadcasted_iota(jnp.int32, (128, tokens.shape[0]), 0)
    first, second = spot == where[0:1, :], spot == where[1:2, :]
    onehot = (first.astype(F32) + second.astype(F32)).astype(BF16)

    @pl.loop(0, blocks)
    def _(c):
        cols = pl.ds(pl.multiple_of(c * TILE, TILE), TILE)
        rows = jnp.dot(onehot, tokens[:, cols], preferred_element_type=F32)
        pk[:, :, cols] = rows.astype(BF16).reshape(8, 16, TILE)

    pl.semaphore_wait(barrier, 13)

    copies = Copies(send, recv)
    dispatch = []
    for s in range(1, 8):
        to = lax.rem(e + s, 8)
        dispatch.append(copies(pk.at[to], dr.at[e], {"expert": to}))
    for copy in dispatch:
        copy.start()
    shared = []
    for src, dst in ((small_gate, wg), (small_up, wu)):
        for s in range(1, 4):
            theirs = pl.ds(units(lax.rem(x + s, 4)), 512)
            shared.append(copies(src.at[:, theirs], dst.at[x], peer(0, s)))
    for copy in shared:
        copy.start()
    down_in = LineGather(copies, neighbour, "z", wo, small_down)
    down_in.start()
    dr[e] = pk[e]

    out_row = lax.broadcasted_iota(jnp.int32, (128, 128), 0)
    in_row = lax.broadcasted_iota(jnp.int32, (128, 128), 1)
    by_kind = ((out_row & 63) >> 3) * 16 + (out_row >> 6) * 8 + (out_row & 7) == in_row
    by_group = ((in_row & 63) >> 3) * 16 + (in_row >> 6) * 8 + (in_row & 7) == out_row
    by_kind, by_group = by_kind.astype(F32).astype(BF16), by_group.astype(F32).astype(BF16)

    for copy in dispatch:
        copy.wait_recv()

    @pl.loop(0, blocks)
    def _(c):
        cols = pl.ds(pl.multiple_of(c * TILE, TILE), TILE)
        inner = pl.ds(pl.multiple_of(lax.rem(c, 4) * TILE, TILE), TILE)
        rows = dr[:, :, cols].reshape(128, TILE)
        rows = jnp.dot(by_kind, rows, preferred_element_type=F32).astype(BF16)
        xg[0, 0:32, cols] = rows[0:32]
        xg[0, 128:160, cols] = rows[32:64]
        sr[lax.div(c, 4), :, inner] = rows[64:128]

    gather = Gather(copies, neighbour, xg)
    gather.step(0)
    spread = []
    for s in range(1, 4):
        spread.append(copies(sr.at[lax.rem(z + s, 4)], xs.at[0, pl.ds(64 * (4 - s), 64)], peer(s, 0)))
    for copy in spread:
        copy.start()
    xs[0, 0:64] = sr[z]

    rows_in = LineGather(copies, neighbour, "x", xs)
    terms_in = LineScatter(copies, neighbour, "z", ps, op, np_)
    acts = LineGather(copies, neighbour, "x", ac)

    def big_scatter(q):
        def row(g, lo, n):
            return xg.at[g, pl.ds(lo, n), pl.ds(q * half, half)]

        return Scatter(copies, neighbour, row, half, ob.at[q], nb.at[q], o2b.at[q], n2b.at[q])

    sums = [big_scatter(0), big_scatter(1)]

    def big_hidden(g, lo, hi):
        @pl.loop(lo, hi)
        def _(j):
            cols = pl.ds(pl.multiple_of(j * 128, 128), 128)
            both = jnp.dot(xg[g], wgu[j], preferred_element_type=F32)
            gate, up = both[:, :128], both[:, 128:]
            hid[g, :, cols] = (gate / (1.0 + jnp.exp(-gate)) * up).astype(BF16)

    def big_terms(g, q):
        @pl.loop(q * half // TILE, (q + 1) * half // TILE)
        def _(c):
            cols = pl.ds(pl.multiple_of(c * TILE, TILE), TILE)
            xg[g, :, cols] = jnp.dot(hid[g], wd[:, cols], preferred_element_type=F32).astype(BF16)

    def small_terms(g):
        rows = jnp.concatenate([xs[r, 64 * g:64 * g + 64] for r in range(4)], axis=0)

        @pl.loop(0, 2)
        def _(c):
            cols = pl.ds(pl.multiple_of(c * TILE, TILE), TILE)
            far = pl.ds(pl.multiple_of(512 + c * TILE, TILE), TILE)
            ps[g, :, cols] = jnp.dot(
                rows, wg[:, :, cols].reshape(1024, TILE), preferred_element_type=F32).astype(BF16)
            ps[g, :, far] = jnp.dot(
                rows, wu[:, :, cols].reshape(1024, TILE), preferred_element_type=F32).astype(BF16)

    def small_hidden():
        @pl.loop(0, 4)
        def _(c):
            cols = pl.ds(pl.multiple_of(c * 128, 128), 128)
            far = pl.ds(pl.multiple_of(512 + c * 128, 128), 128)
            gate, up = terms_in.total(cols), terms_in.total(far)
            act = gate / (1.0 + jnp.exp(-gate)) * up
            twice = jnp.logical_and(c == 0, x >= 2)
            act = jnp.where(twice, 0.0, act).astype(BF16)
            for r in range(4):
                here = pl.ds(pl.multiple_of(lax.rem(x + r, 4) * 64, 64), 64)
                ac[0, here, cols] = act[64 * r:64 * r + 64]

    def small_back():
        @pl.loop(0, 4)
        def _(c):
            rows = jnp.zeros((256, TILE), F32)
            for k in range(4):
                some = pl.ds(units(lax.rem(x + k, 4)), 512)
                rows += jnp.dot(ac[k], wo[c, some, :], preferred_element_type=F32)
            cols = pl.ds(pl.multiple_of(c * TILE, TILE), TILE)
            pd[:, :, cols] = rows.astype(BF16).reshape(4, 64, TILE)

    gather.step(1)
    for copy in spread:
        copy.wait_recv()
    rows_in.start()
    gather.step(2)
    gather.step(3)
    for load in tile_loads:
        load.wait()
    big_hidden(0, 0, 3)
    gather.step(4)
    rows_in.relay()
    big_hidden(0, 3, tiles)
    gather.step(5)
    down_in.relay()
    rows_in.finish()
    for load in loads[:2]:
        load.wait()
    for copy in shared:
        copy.wait_recv()
    small_terms(2)
    for copy in terms_in.far:
        copy.start()
    small_terms(1)
    terms_in.early[0].start()
    small_terms(3)
    terms_in.early[1].start()
    small_terms(0)
    gather.step(6)
    big_hidden(1, 0, tiles)
    terms_in.relay()
    big_hidden(3, 0, tiles)
    loads[3].wait()
    gather.sent(True)
    big_terms(1, 0)
    sums[0].early(1)
    big_terms(3, 0)
    sums[0].early(3)
    terms_in.finish()
    small_hidden()
    acts.start()
    gather.step(7)
    big_hidden(2, 0, tiles)
    big_terms(2, 0)
    sums[0].opposite()
    acts.relay()
    big_terms(2, 1)
    sums[1].opposite()
    big_terms(1, 1)
    sums[1].early(1)
    big_terms(3, 1)
    sums[1].early(3)
    gather.sent(False)
    sums[0].step(1)
    acts.finish()
    down_in.finish()
    loads[2].wait()
    small_back()
    home = []
    for s in range(1, 4):
        home.append(copies(pd.at[lax.rem(x + s, 4)], sb.at[x], peer(0, s)))
    for copy in home:
        copy.start()
    sb[x] = pd[x]
    big_terms(0, 0)
    big_terms(0, 1)
    sums[1].step(1)
    sums[0].step(2)
    sums[1].step(2)

    mix = jnp.where(first, weights[0:1, :], 0.0) + jnp.where(second, weights[1:2, :], 0.0)
    mix = mix.T
    coarse = mix.astype(BF16)
    fine = (mix - coarse.astype(F32)).astype(BF16)
    for copy in dispatch:
        copy.wait_send()

    returned = [[], []]
    for q in (0, 1):
        for s in range(1, 8):
            to = lax.rem(e + s, 8)
            part = pl.ds(q * half, half)
            returned[q].append(copies(pk.at[to, :, part], hm.at[e, :, part], {"expert": to}))

    sums[0].step(3)
    sums[1].step(3)
    for q in (0, 1):
        sums[q].step(4)
        if q == 0:
            for copy in home:
                copy.wait_recv()

        @pl.loop(0, half // TILE)
        def _(c):
            cols = pl.ds(pl.multiple_of(c * TILE, TILE), TILE)
            far = pl.ds(pl.multiple_of(q * half + c * TILE, TILE), TILE)
            steps = lax.rem(2 * q + lax.div(c, 4) - z + 4, 4)
            inner = pl.ds(pl.multiple_of(steps * TILE, TILE), TILE)
            rows = jnp.concatenate(
                [sums[q].total(h, cols).astype(BF16) for h in (0, 1)]
                + [sb[lax.rem(c, 4), :, inner]], axis=0)
            rows = jnp.dot(by_group, rows, preferred_element_type=F32).astype(BF16)
            pk[:, :, far] = rows.reshape(8, 16, TILE)

        for copy in returned[q]:
            copy.start()
        part = slice(q * half, (q + 1) * half)
        hm[e, :, part] = pk[e, :, part]

    for q in (0, 1):
        for copy in returned[q]:
            copy.wait_recv()

        @pl.loop(q * half // TILE, (q + 1) * half // TILE)
        def _(c):
            cols = pl.ds(pl.multiple_of(c * TILE, TILE), TILE)
            rows = hm[:, :, cols].reshape(128, TILE)
            total = jnp.dot(coarse, rows, preferred_element_type=F32)
            total += jnp.dot(fine, rows, preferred_element_type=F32)
            out[:, cols] = total.astype(BF16)

    for copy in shared + spread + home + returned[0] + returned[1]:
        copy.wait_send()
    for group in (down_in, rows_in, terms_in, acts, sums[0], sums[1]):
        group.sent()


def shards(
    tokens, expert_ids, slots, combine_weights,
    big_gate, big_up, big_down, small_gate, small_up, small_down,
):
    tok, width = tokens.shape
    hidden = big_gate.shape[2]
    small = small_gate.shape[2]
    half = width // 2
    vmem = pl.BlockSpec(memory_space=pltpu.VMEM)
    hbm = pl.BlockSpec(memory_space=pl.ANY)

    def buf(*shape):
        return pltpu.VMEM(shape, BF16)

    n_copies = 7 + 6 + 4 + 32 + 3 + 4 + 6 + 4 + 40 + 3 + 14
    return pl.pallas_call(
        kernel,
        out_shape=jax.ShapeDtypeStruct((tok, width), BF16),
        in_specs=[vmem] * 4 + [hbm] * 6,
        out_specs=vmem,
        scratch_shapes=[
            buf(8, 16, width), buf(8, 16, width), buf(8, 16, width),
            buf(4, 256, width), buf(hidden // 128, width, 256), buf(hidden, width), buf(4, 256, hidden),
            buf(2, 2, 2, 64, half), buf(2, 2, 2, 128, half), buf(2, 2, 2, 16, half), buf(2, 2, 2, 32, half),
            buf(4, 64, 1024), buf(4, 256, 1024), buf(4, 256, 512), buf(4, 256, 512), buf(4, small, 256),
            buf(4, 256, 1024), buf(2, 128, 1024), buf(2, 256, 1024),
            buf(4, 256, 512),
            buf(4, 64, 1024), buf(4, 64, 1024),
            pltpu.SemaphoreType.DMA((n_copies,)),
            pltpu.SemaphoreType.DMA((n_copies,)),
            pltpu.SemaphoreType.DMA((4,)),
            pltpu.SemaphoreType.DMA((hidden // 128, 2)),
        ],
        compiler_params=pltpu.CompilerParams(
            collective_id=0, has_side_effects=True, vmem_limit_bytes=62 * 1024 * 1024
        ),
        cost_estimate=pl.CostEstimate(
            flops=6 * 1024 * width * hidden + 6 * 1024 * TILE * small,
            bytes_accessed=6 * width * hidden + 6 * TILE * small,
            transcendentals=1024 * hidden,
        ),
        name="moe_layer",
    )(
        expert_ids.T, slots.T, combine_weights.T, tokens,
        big_gate[0], big_up[0], big_down[0], small_gate[0], small_up[0], small_down[0],
    )


def solution(mesh):
    return jax.shard_map(
        shards,
        mesh=mesh,
        in_specs=(
            P(("expert", "tensor"), None),
            P(("expert", "tensor"), None),
            P(("expert", "tensor"), None),
            P(("expert", "tensor"), None),
            P("expert", None, "tensor"),
            P("expert", None, "tensor"),
            P("expert", "tensor", None),
            P("expert", "tensor", None),
            P("expert", "tensor", None),
            P("expert", None, "tensor"),
        ),
        out_specs=P(("expert", "tensor"), None),
        check_vma=False,
    )
```

```python
import jax
import jax.numpy as jnp
from jax import lax
from jax.experimental import pallas as pl
from jax.experimental.pallas import tpu as pltpu
from jax.sharding import PartitionSpec as P

F32, BF16 = jnp.float32, jnp.bfloat16
MESH = pl.DeviceIdType.MESH
TILE = 256
AXES = (("x", "z"), ("z", "x"))


def add_into(dst, parts, rows, width):
    step = min(width, 512)

    @pl.loop(0, width // step)
    def _(c):
        cols = pl.ds(pl.multiple_of(c * step, step), step)
        total = dst[:, cols].astype(F32)
        for part in parts:
            total += part[:, cols].astype(F32)
        dst[:, cols] = total.astype(BF16)


class Copies:
    def __init__(self, send, recv):
        self.send, self.recv, self.used = send, recv, 0

    def __call__(self, src, dst, device):
        k = self.used
        self.used += 1
        return pltpu.make_async_remote_copy(
            src_ref=src, dst_ref=dst, send_sem=self.send.at[k], recv_sem=self.recv.at[k],
            device_id=device, device_id_type=MESH,
        )


class Gather:
    def __init__(self, copies, neighbour, buf):
        self.c = c = {}
        for h, (first, second) in enumerate(AXES):
            def row(g, r, lo=0, n=32):
                return buf.at[g, pl.ds(128 * h + 32 * r + lo, n)]

            c[h, "a", 1] = copies(row(0, 0), row(0, 3), neighbour(first, 1))
            c[h, "a", 3] = copies(row(0, 0), row(0, 1), neighbour(first, 3))
            c[h, "f", 1] = copies(row(0, 3, 0, 16), row(0, 2, 0, 16), neighbour(first, 1))
            c[h, "f", 3] = copies(row(0, 1, 16, 16), row(0, 2, 16, 16), neighbour(first, 3))
            for r in range(4):
                c[h, "b", 1, r] = copies(row(0, r), row(3, r), neighbour(second, 1))
                c[h, "b", 3, r] = copies(row(0, r), row(1, r), neighbour(second, 3))
            for r in (0, 1):
                c[h, "g", 1, r] = copies(row(3, r), row(2, r), neighbour(second, 1))
            for r in (2, 3):
                c[h, "g", 3, r] = copies(row(1, r), row(2, r), neighbour(second, 3))

    def step(self, number):
        c = self.c
        for h in (0, 1):
            def go(*keys):
                for key in keys:
                    c[(h, *key)].start()

            def got(*keys):
                for key in keys:
                    c[(h, *key)].wait_recv()

            if number == 0:
                go(("a", 1), ("a", 3), ("b", 1, 0), ("b", 3, 0))
            elif number == 1:
                got(("a", 1))
                go(("f", 1), ("b", 1, 3), ("b", 3, 3))
                got(("a", 3))
                go(("f", 3), ("b", 1, 1), ("b", 3, 1))
            elif number == 2:
                got(("b", 1, 0))
                go(("g", 1, 0))
            elif number == 3:
                got(("f", 1), ("f", 3))
                go(("b", 1, 2), ("b", 3, 2))
            elif number == 4:
                got(("b", 1, 1))
                go(("g", 1, 1))
                got(("b", 3, 3))
                go(("g", 3, 3))
            elif number == 5:
                got(("b", 3, 2))
                go(("g", 3, 2))
            elif number == 6:
                got(("b", 1, 2), ("b", 1, 3), ("b", 3, 0), ("b", 3, 1))
            else:
                got(("g", 1, 0), ("g", 1, 1), ("g", 3, 2), ("g", 3, 3))

    def sent(self, relayed):
        for key, copy in self.c.items():
            if (key[1] == "g") == relayed:
                copy.wait_send()


class LineGather:
    def __init__(self, copies, neighbour, axis, buf, own=None):
        middle = buf.shape[1] // 2
        low, high = pl.ds(0, middle), pl.ds(middle, middle)
        up, down = neighbour(axis, 1), neighbour(axis, 3)
        own = buf.at[0] if own is None else own
        self.out = [copies(own, buf.at[3], up), copies(own, buf.at[1], down)]
        self.on = [
            copies(buf.at[3, low], buf.at[2, low], up), copies(buf.at[1, high], buf.at[2, high], down)
        ]

    def start(self):
        for copy in self.out:
            copy.start()

    def relay(self):
        for first, second in zip(self.out, self.on):
            first.wait_recv()
            second.start()

    def finish(self):
        for copy in self.on:
            copy.wait_recv()

    def sent(self):
        for copy in self.out + self.on:
            copy.wait_send()


class LineScatter:
    def __init__(self, copies, neighbour, axis, buf, o, n):
        low, high = pl.ds(0, 128), pl.ds(128, 128)
        up, down = neighbour(axis, 1), neighbour(axis, 3)
        self.buf, self.o, self.n = buf, o, n
        self.low, self.high = low, high
        self.far = [copies(buf.at[2, low], o.at[0], up), copies(buf.at[2, high], o.at[1], down)]
        self.early = [copies(buf.at[1, high], n.at[0, high], up), copies(buf.at[3, low], n.at[1, low], down)]
        self.late = [copies(buf.at[1, low], n.at[0, low], up), copies(buf.at[3, high], n.at[1, high], down)]

    def relay(self):
        width = self.o.shape[-1]
        self.far[0].wait_recv()
        add_into(self.buf.at[1, self.low], [self.o.at[0]], 128, width)
        self.late[0].start()
        self.far[1].wait_recv()
        add_into(self.buf.at[3, self.high], [self.o.at[1]], 128, width)
        self.late[1].start()

    def finish(self):
        for copy in self.early + self.late:
            copy.wait_recv()

    def total(self, cols):
        return self.buf[0, :, cols].astype(F32) + self.n[0, :, cols].astype(F32) + self.n[1, :, cols].astype(F32)

    def sent(self):
        for copy in self.far + self.early + self.late:
            copy.wait_send()


class Scatter:
    def __init__(self, copies, neighbour, row, width, o, n, o2, n2):
        self.row, self.width = row, width
        self.o, self.n, self.o2, self.n2 = o, n, o2, n2
        self.c = c = {}
        for h, (second, first) in enumerate(AXES):
            b = 128 * h
            c[h, "o", 1] = copies(row(2, b, 64), o.at[h, 0], neighbour(first, 1))
            c[h, "o", 3] = copies(row(2, b + 64, 64), o.at[h, 1], neighbour(first, 3))
            c[h, "e", 1] = copies(row(1, b + 64, 64), n.at[h, 0, pl.ds(64, 64)], neighbour(first, 1))
            c[h, "e", 3] = copies(row(3, b, 64), n.at[h, 1, pl.ds(0, 64)], neighbour(first, 3))
            c[h, "l", 1] = copies(row(1, b, 64), n.at[h, 0, pl.ds(0, 64)], neighbour(first, 1))
            c[h, "l", 3] = copies(row(3, b + 64, 64), n.at[h, 1, pl.ds(64, 64)], neighbour(first, 3))
            c[h, "p", 1] = copies(row(0, b + 64, 16), o2.at[h, 0], neighbour(second, 1))
            c[h, "p", 3] = copies(row(0, b + 80, 16), o2.at[h, 1], neighbour(second, 3))
            c[h, "q", 1] = copies(row(0, b + 32, 32), n2.at[h, 0], neighbour(second, 1))
            c[h, "q", 3] = copies(row(0, b + 96, 32), n2.at[h, 1], neighbour(second, 3))

    def opposite(self):
        for h in (0, 1):
            self.c[h, "o", 1].start()
            self.c[h, "o", 3].start()

    def early(self, way):
        for h in (0, 1):
            self.c[h, "e", way].start()

    def step(self, number):
        c, row, width = self.c, self.row, self.width
        for h in (0, 1):
            b = 128 * h
            if number == 1:
                c[h, "o", 1].wait_recv()
                add_into(row(1, b, 64), [self.o.at[h, 0]], 64, width)
                c[h, "l", 1].start()
                c[h, "o", 3].wait_recv()
                add_into(row(3, b + 64, 64), [self.o.at[h, 1]], 64, width)
                c[h, "l", 3].start()
            elif number == 2:
                for way in (1, 3):
                    c[h, "e", way].wait_recv()
                    c[h, "l", way].wait_recv()
                add_into(row(0, b, 128), [self.n.at[h, 0], self.n.at[h, 1]], 128, width)
                c[h, "p", 1].start()
                c[h, "p", 3].start()
            elif number == 3:
                c[h, "p", 1].wait_recv()
                add_into(row(0, b + 32, 16), [self.o2.at[h, 0]], 16, width)
                c[h, "q", 1].start()
                c[h, "p", 3].wait_recv()
                add_into(row(0, b + 112, 16), [self.o2.at[h, 1]], 16, width)
                c[h, "q", 3].start()
            else:
                c[h, "q", 1].wait_recv()
                c[h, "q", 3].wait_recv()

    def total(self, h, cols):
        own = self.row(0, 128 * h, 32)[:, cols].astype(F32)
        return own + self.n2[h, 0, :, cols].astype(F32) + self.n2[h, 1, :, cols].astype(F32)

    def sent(self):
        for copy in self.c.values():
            copy.wait_send()


def kernel(
    ids, slots, weights, tokens, big_gate, big_up, big_down, small_gate, small_up, small_down,
    out,
    pk, dr, hm, xg, wgu, wd, hid, ob, nb, o2b, n2b,
    sr, xs, wg, wu, wo, ps, op, np_, ac, pd, sb,
    send, recv, local, tile_sem,
):
    width = tokens.shape[1]
    hidden = wd.shape[0]
    tiles = hidden // 128
    blocks = width // TILE
    half = width // 2
    e = lax.axis_index("expert")
    t = lax.axis_index("tensor")
    z, x = lax.div(t, 4), lax.rem(t, 4)

    def peer(sz, sx):
        return {"tensor": lax.rem(z + sz, 4) * 4 + lax.rem(x + sx, 4)}

    def neighbour(axis, s):
        return peer(s, 0) if axis == "z" else peer(0, s)

    barrier = pltpu.get_barrier_semaphore()
    for s in range(1, 8):
        pl.semaphore_signal(barrier, inc=1, device_id={"expert": lax.rem(e + s, 8)}, device_id_type=MESH)
    for s in range(1, 4):
        for axis in ("x", "z"):
            pl.semaphore_signal(barrier, inc=1, device_id=neighbour(axis, s), device_id_type=MESH)

    def units(place):
        return pl.multiple_of(128 * (4 * place - lax.max(place - 1, 0)), 128)

    mine = pl.ds(units(x), 512)
    loads = [
        pltpu.make_async_copy(src, dst, local.at[k])
        for k, (src, dst) in enumerate((
            (small_gate.at[:, mine], wg.at[x]), (small_up.at[:, mine], wu.at[x]),
            (small_down, wo.at[0]), (big_down, wd),
        ))
    ]
    tile_loads = []
    for j in range(tiles):
        cols = pl.ds(j * 128, 128)
        tile_loads.append(pltpu.make_async_copy(big_gate.at[:, cols], wgu.at[j, :, pl.ds(0, 128)], tile_sem.at[j, 0]))
        tile_loads.append(pltpu.make_async_copy(big_up.at[:, cols], wgu.at[j, :, pl.ds(128, 128)], tile_sem.at[j, 1]))
    for load in loads + tile_loads:
        load.start()

    where = (ids[...] & 7) * 16 + (ids[...] >> 3) * 8 + slots[...]
    spot = lax.broadcasted_iota(jnp.int32, (128, tokens.shape[0]), 0)
    first, second = spot == where[0:1, :], spot == where[1:2, :]
    onehot = (first.astype(F32) + second.astype(F32)).astype(BF16)

    @pl.loop(0, blocks)
    def _(c):
        cols = pl.ds(pl.multiple_of(c * TILE, TILE), TILE)
        rows = jnp.dot(onehot, tokens[:, cols], preferred_element_type=F32)
        pk[:, :, cols] = rows.astype(BF16).reshape(8, 16, TILE)

    pl.semaphore_wait(barrier, 13)

    copies = Copies(send, recv)
    dispatch = []
    for s in range(1, 8):
        to = lax.rem(e + s, 8)
        dispatch.append(copies(pk.at[to], dr.at[e], {"expert": to}))
    for copy in dispatch:
        copy.start()
    shared = []
    for src, dst in ((small_gate, wg), (small_up, wu)):
        for s in range(1, 4):
            theirs = pl.ds(units(lax.rem(x + s, 4)), 512)
            shared.append(copies(src.at[:, theirs], dst.at[x], peer(0, s)))
    for copy in shared:
        copy.start()
    down_in = LineGather(copies, neighbour, "z", wo, small_down)
    dr[e] = pk[e]

    out_row = lax.broadcasted_iota(jnp.int32, (128, 128), 0)
    in_row = lax.broadcasted_iota(jnp.int32, (128, 128), 1)
    by_kind = ((out_row & 63) >> 3) * 16 + (out_row >> 6) * 8 + (out_row & 7) == in_row
    by_group = ((in_row & 63) >> 3) * 16 + (in_row >> 6) * 8 + (in_row & 7) == out_row
    by_kind, by_group = by_kind.astype(F32).astype(BF16), by_group.astype(F32).astype(BF16)

    for copy in dispatch:
        copy.wait_recv()

    @pl.loop(0, blocks)
    def _(c):
        cols = pl.ds(pl.multiple_of(c * TILE, TILE), TILE)
        inner = pl.ds(pl.multiple_of(lax.rem(c, 4) * TILE, TILE), TILE)
        rows = dr[:, :, cols].reshape(128, TILE)
        rows = jnp.dot(by_kind, rows, preferred_element_type=F32).astype(BF16)
        xg[0, 0:32, cols] = rows[0:32]
        xg[0, 128:160, cols] = rows[32:64]
        sr[lax.div(c, 4), :, inner] = rows[64:128]

    gather = Gather(copies, neighbour, xg)
    gather.step(0)
    spread = []
    for s in range(1, 4):
        spread.append(copies(sr.at[lax.rem(z + s, 4)], xs.at[0, pl.ds(64 * (4 - s), 64)], peer(s, 0)))
    for copy in spread:
        copy.start()
    xs[0, 0:64] = sr[z]

    rows_in = LineGather(copies, neighbour, "x", xs)
    terms_in = LineScatter(copies, neighbour, "z", ps, op, np_)
    acts = LineGather(copies, neighbour, "x", ac)

    def big_scatter(q):
        def row(g, lo, n):
            return xg.at[g, pl.ds(lo, n), pl.ds(q * half, half)]

        return Scatter(copies, neighbour, row, half, ob.at[q], nb.at[q], o2b.at[q], n2b.at[q])

    sums = [big_scatter(0), big_scatter(1)]

    def big_hidden(g, lo, hi):
        @pl.loop(lo, hi)
        def _(j):
            cols = pl.ds(pl.multiple_of(j * 128, 128), 128)
            both = jnp.dot(xg[g], wgu[j], preferred_element_type=F32)
            gate, up = both[:, :128], both[:, 128:]
            hid[g, :, cols] = (gate / (1.0 + jnp.exp(-gate)) * up).astype(BF16)

    def big_terms(g, q):
        @pl.loop(q * half // TILE, (q + 1) * half // TILE)
        def _(c):
            cols = pl.ds(pl.multiple_of(c * TILE, TILE), TILE)
            xg[g, :, cols] = jnp.dot(hid[g], wd[:, cols], preferred_element_type=F32).astype(BF16)

    def small_terms(g):
        rows = jnp.concatenate([xs[r, 64 * g:64 * g + 64] for r in range(4)], axis=0)

        @pl.loop(0, 2)
        def _(c):
            cols = pl.ds(pl.multiple_of(c * TILE, TILE), TILE)
            far = pl.ds(pl.multiple_of(512 + c * TILE, TILE), TILE)
            ps[g, :, cols] = jnp.dot(
                rows, wg[:, :, cols].reshape(1024, TILE), preferred_element_type=F32).astype(BF16)
            ps[g, :, far] = jnp.dot(
                rows, wu[:, :, cols].reshape(1024, TILE), preferred_element_type=F32).astype(BF16)

    def small_hidden():
        @pl.loop(0, 4)
        def _(c):
            cols = pl.ds(pl.multiple_of(c * 128, 128), 128)
            far = pl.ds(pl.multiple_of(512 + c * 128, 128), 128)
            gate, up = terms_in.total(cols), terms_in.total(far)
            act = gate / (1.0 + jnp.exp(-gate)) * up
            twice = jnp.logical_and(c == 0, x >= 2)
            act = jnp.where(twice, 0.0, act).astype(BF16)
            for r in range(4):
                here = pl.ds(pl.multiple_of(lax.rem(x + r, 4) * 64, 64), 64)
                ac[0, here, cols] = act[64 * r:64 * r + 64]

    def small_back():
        @pl.loop(0, 4)
        def _(c):
            rows = jnp.zeros((256, TILE), F32)
            for k in range(4):
                some = pl.ds(units(lax.rem(x + k, 4)), 512)
                rows += jnp.dot(ac[k], wo[c, some, :], preferred_element_type=F32)
            cols = pl.ds(pl.multiple_of(c * TILE, TILE), TILE)
            pd[:, :, cols] = rows.astype(BF16).reshape(4, 64, TILE)

    gather.step(1)
    for copy in spread:
        copy.wait_recv()
    rows_in.start()
    gather.step(2)
    gather.step(3)
    down_in.start()
    for load in tile_loads:
        load.wait()
    loads[3].wait()
    big_hidden(0, 0, 3)
    gather.step(4)
    big_hidden(0, 3, tiles)
    gather.step(5)
    rows_in.relay()
    gather.step(6)
    big_hidden(1, 0, tiles)
    rows_in.finish()
    for load in loads[:2]:
        load.wait()
    for copy in shared:
        copy.wait_recv()
    small_terms(2)
    for copy in terms_in.far:
        copy.start()
    small_terms(1)
    terms_in.early[0].start()
    small_terms(3)
    terms_in.early[1].start()
    gather.step(7)
    big_hidden(2, 0, tiles)
    gather.sent(True)
    big_terms(2, 0)
    sums[0].opposite()
    big_terms(2, 1)
    sums[1].opposite()
    down_in.relay()
    terms_in.relay()
    small_terms(0)
    big_terms(1, 0)
    sums[0].early(1)
    big_terms(1, 1)
    sums[1].early(1)
    big_hidden(3, 0, tiles)
    big_terms(3, 0)
    sums[0].early(3)
    big_terms(3, 1)
    sums[1].early(3)
    terms_in.finish()
    small_hidden()
    acts.start()
    sums[0].step(1)
    sums[1].step(1)
    gather.sent(False)
    big_terms(0, 0)
    acts.relay()
    big_terms(0, 1)
    sums[0].step(2)
    acts.finish()
    down_in.finish()
    loads[2].wait()
    small_back()
    home = []
    for s in range(1, 4):
        home.append(copies(pd.at[lax.rem(x + s, 4)], sb.at[x], peer(0, s)))
    for copy in home:
        copy.start()
    sb[x] = pd[x]
    sums[1].step(2)
    sums[0].step(3)
    sums[1].step(3)

    mix = jnp.where(first, weights[0:1, :], 0.0) + jnp.where(second, weights[1:2, :], 0.0)
    mix = mix.T
    coarse = mix.astype(BF16)
    fine = (mix - coarse.astype(F32)).astype(BF16)
    for copy in dispatch:
        copy.wait_send()

    returned = [[], []]
    for q in (0, 1):
        for s in range(1, 8):
            to = lax.rem(e + s, 8)
            part = pl.ds(q * half, half)
            returned[q].append(copies(pk.at[to, :, part], hm.at[e, :, part], {"expert": to}))

    for q in (0, 1):
        sums[q].step(4)
        if q == 0:
            for copy in home:
                copy.wait_recv()

        @pl.loop(0, half // TILE)
        def _(c):
            cols = pl.ds(pl.multiple_of(c * TILE, TILE), TILE)
            far = pl.ds(pl.multiple_of(q * half + c * TILE, TILE), TILE)
            steps = lax.rem(2 * q + lax.div(c, 4) - z + 4, 4)
            inner = pl.ds(pl.multiple_of(steps * TILE, TILE), TILE)
            rows = jnp.concatenate(
                [sums[q].total(h, cols).astype(BF16) for h in (0, 1)]
                + [sb[lax.rem(c, 4), :, inner]], axis=0)
            rows = jnp.dot(by_group, rows, preferred_element_type=F32).astype(BF16)
            pk[:, :, far] = rows.reshape(8, 16, TILE)

        for copy in returned[q]:
            copy.start()
        part = slice(q * half, (q + 1) * half)
        hm[e, :, part] = pk[e, :, part]

    for q in (0, 1):
        for copy in returned[q]:
            copy.wait_recv()

        @pl.loop(q * half // TILE, (q + 1) * half // TILE)
        def _(c):
            cols = pl.ds(pl.multiple_of(c * TILE, TILE), TILE)
            rows = hm[:, :, cols].reshape(128, TILE)
            total = jnp.dot(coarse, rows, preferred_element_type=F32)
            total += jnp.dot(fine, rows, preferred_element_type=F32)
            out[:, cols] = total.astype(BF16)

    for copy in shared + spread + home + returned[0] + returned[1]:
        copy.wait_send()
    for group in (down_in, rows_in, terms_in, acts, sums[0], sums[1]):
        group.sent()


def shards(
    tokens, expert_ids, slots, combine_weights,
    big_gate, big_up, big_down, small_gate, small_up, small_down,
):
    tok, width = tokens.shape
    hidden = big_gate.shape[2]
    small = small_gate.shape[2]
    half = width // 2
    vmem = pl.BlockSpec(memory_space=pltpu.VMEM)
    hbm = pl.BlockSpec(memory_space=pl.ANY)

    def buf(*shape):
        return pltpu.VMEM(shape, BF16)

    n_copies = 7 + 6 + 4 + 32 + 3 + 4 + 6 + 4 + 40 + 3 + 14
    return pl.pallas_call(
        kernel,
        out_shape=jax.ShapeDtypeStruct((tok, width), BF16),
        in_specs=[vmem] * 4 + [hbm] * 6,
        out_specs=vmem,
        scratch_shapes=[
            buf(8, 16, width), buf(8, 16, width), buf(8, 16, width),
            buf(4, 256, width), buf(hidden // 128, width, 256), buf(hidden, width), buf(4, 256, hidden),
            buf(2, 2, 2, 64, half), buf(2, 2, 2, 128, half), buf(2, 2, 2, 16, half), buf(2, 2, 2, 32, half),
            buf(4, 64, 1024), buf(4, 256, 1024), buf(4, 256, 512), buf(4, 256, 512), buf(4, small, 256),
            buf(4, 256, 1024), buf(2, 128, 1024), buf(2, 256, 1024),
            buf(4, 256, 512),
            buf(4, 64, 1024), buf(4, 64, 1024),
            pltpu.SemaphoreType.DMA((n_copies,)),
            pltpu.SemaphoreType.DMA((n_copies,)),
            pltpu.SemaphoreType.DMA((4,)),
            pltpu.SemaphoreType.DMA((hidden // 128, 2)),
        ],
        compiler_params=pltpu.CompilerParams(
            collective_id=0, has_side_effects=True, vmem_limit_bytes=62 * 1024 * 1024
        ),
        cost_estimate=pl.CostEstimate(
            flops=6 * 1024 * width * hidden + 6 * 1024 * TILE * small,
            bytes_accessed=6 * width * hidden + 6 * TILE * small,
            transcendentals=1024 * hidden,
        ),
        name="moe_layer",
    )(
        expert_ids.T, slots.T, combine_weights.T, tokens,
        big_gate[0], big_up[0], big_down[0], small_gate[0], small_up[0], small_down[0],
    )


def solution(mesh):
    return jax.shard_map(
        shards,
        mesh=mesh,
        in_specs=(
            P(("expert", "tensor"), None),
            P(("expert", "tensor"), None),
            P(("expert", "tensor"), None),
            P(("expert", "tensor"), None),
            P("expert", None, "tensor"),
            P("expert", None, "tensor"),
            P("expert", "tensor", None),
            P("expert", "tensor", None),
            P("expert", "tensor", None),
            P("expert", None, "tensor"),
        ),
        out_specs=P(("expert", "tensor"), None),
        check_vma=False,
    )
```
